768 devices in a mesh: row: 24 (over z_lo, y), rep: 32 (over z_hi, x, core).
Axes of the slice: x: 4, y: 8, z: 12 (z_hi: 4, z_lo: 3; z = z_hi * 3 + z_lo), core: 2. Of those that a mesh axis runs over, the one named last changes fastest.
Arguments:
- features: bfloat16 [12288, 128], P('row'), may hold values from -6 to 6
- weight: bfloat16 [128, 256], replicated, may hold values from -0.5 to 0.5
- cotangent: bfloat16 [12288, 256], P('row'), may hold values from -6 to 6
- adj_values: bfloat16 [98304, 128, 128], P(('row', 'rep')), as said below
- block_rows: int32 [98304], P(('row', 'rep')), may hold values from 0 to 3
- block_cols: int32 [98304], P(('row', 'rep')), may hold values from 0 to 95
- block_live: int32 [98304], P(('row', 'rep')), may hold values from 0 to 1
Outputs:
- out_rows: bfloat16 [12288, 256], P('row')
- grad_weight: float32 [128, 256], replicated
- grad_features: bfloat16 [12288, 128], P('row')
The draws below stay inside these ranges and needn't reach their ends.
Inputs may be any that keep to these rules, and one draw needn't show every extreme that they name: `adj_values`: the matrix assembled from the live tiles equals its transpose.
All inputs are finite; a program needn't handle non-finite values.
Results may differ from the reference program's by a relative error of at most 0.0051.
Values may be sent and summed in bfloat16 or wider, within the bound.
No kernel may reach another device: no remote copies, remote signals or barrier semaphores. Data moves between devices by JAX's collectives and lax.ppermute only.
A program may use at most 128 MiB of HBM per device.

```python
import jax
import jax.numpy as jnp
from jax import lax

D_IN = 128
D_OUT = 256
TILE = 128
OWNER_ROW_BLOCKS = 4
KB = 128
NODES = 12288
TILE_SLOT_TOTAL = 98304
N_ROW = 24
N_REP = 32


def pattern(key):
    half_slots = KB // 2
    subkeys = jax.random.split(key, 6)
    shifts = jax.random.randint(subkeys[0], (N_REP, half_slots), 0, N_ROW)
    sender_row = jax.random.randint(subkeys[1], (N_ROW, N_REP, half_slots), 0, OWNER_ROW_BLOCKS)
    sender_column = jax.random.randint(subkeys[2], (N_ROW, N_REP, half_slots), 0, OWNER_ROW_BLOCKS)
    levels = jax.random.randint(subkeys[3], (N_ROW * N_REP,), 2, 9)
    full_device = jax.random.randint(subkeys[4], (), 0, N_ROW * N_REP)
    levels = jnp.where(jnp.arange(N_ROW * N_REP) == full_device, 8, levels).reshape(N_ROW, N_REP, 1)
    coin_flips = jax.random.randint(subkeys[5], (N_ROW, N_REP, half_slots), 0, 8)
    sender_live = (coin_flips < levels).astype(jnp.int32)
    owner_ids = jnp.arange(N_ROW, dtype=jnp.int32).reshape(N_ROW, 1, 1)
    member_index_list = jnp.arange(N_REP, dtype=jnp.int32).reshape(1, N_REP, 1)
    slot_index_list = jnp.arange(half_slots, dtype=jnp.int32).reshape(1, 1, half_slots)
    receiver_nodes = (owner_ids + shifts[None]) % N_ROW
    sender_nodes = (owner_ids - shifts[None] + N_ROW) % N_ROW
    reflected_row = sender_column[sender_nodes, member_index_list, slot_index_list]
    reflected_column = sender_nodes * OWNER_ROW_BLOCKS + sender_row[sender_nodes, member_index_list, slot_index_list]
    reflected_live = sender_live[sender_nodes, member_index_list, slot_index_list]
    every_row = jnp.concatenate([sender_row, reflected_row], axis=2).reshape(TILE_SLOT_TOTAL).astype(jnp.int32)
    every_column = jnp.concatenate([receiver_nodes * OWNER_ROW_BLOCKS + sender_column, reflected_column], axis=2).reshape(TILE_SLOT_TOTAL).astype(jnp.int32)
    every_live_flag = jnp.concatenate([sender_live, reflected_live], axis=2).reshape(TILE_SLOT_TOTAL).astype(jnp.int32)
    return (every_row, every_column, every_live_flag, sender_nodes, member_index_list, slot_index_list)


def draw_adj_values(key, part):
    layout = pattern(key)
    key = jax.random.fold_in(key, 11)
    sender_nodes, member_index_list, slot_index_list = (layout[3], layout[4], layout[5])
    half_slots = KB // 2
    spread = (N_REP * KB * TILE * 0.6 / OWNER_ROW_BLOCKS) ** (-0.5)
    shape_all = (N_ROW, N_REP, half_slots, TILE, TILE)
    base_tiles = jax.random.normal(key, shape_all, jnp.float32) * spread
    mirror = jnp.swapaxes(base_tiles[sender_nodes, member_index_list, slot_index_list], -1, -2)
    tiles_all = jnp.concatenate([base_tiles, mirror], axis=2).reshape(TILE_SLOT_TOTAL, TILE, TILE)
    return tiles_all.astype(jnp.bfloat16)


def draw_block_rows(key, part):
    layout = pattern(key)
    return layout[0]


def draw_block_cols(key, part):
    layout = pattern(key)
    return layout[1]


def draw_block_live(key, part):
    layout = pattern(key)
    return layout[2]


def level_of(rng, extent, pieces, smallest, largest):
    gain = 1.0
    for axis_at, blocks in pieces:
        steps = jax.random.uniform(jax.random.fold_in(jax.random.fold_in(rng, 6), axis_at), (blocks,), jnp.float32, smallest / len(pieces), largest / len(pieces))
        gain = gain * jnp.repeat(jnp.exp(steps), extent[axis_at] // blocks).reshape((-1,) + (1,) * (len(extent) - 1 - axis_at))
    return gain


def scatter_about(key, dims, scale, most, shards=(), kind=jnp.bfloat16):
    level = level_of(key, dims, shards, -0.22, 0.18) if shards else 1.0
    array = jax.random.normal(key, dims, jnp.float32) * scale * level
    return jnp.minimum(jnp.maximum(array, -most), most).astype(kind)


def setup_inputs(seed: int = 0) -> dict:
    key_of = jax.random.split(jax.random.key(seed), 8)
    return {
        "features": scatter_about(key_of[0], (NODES, D_IN), 1.0, 6.0, ((0, 24),)),
        "weight": scatter_about(key_of[1], (D_IN, D_OUT), D_IN ** -0.5, 0.5),
        "cotangent": scatter_about(key_of[2], (NODES, D_OUT), 1.0, 6.0, ((0, 24),)),
        "adj_values": draw_adj_values(jax.random.fold_in(key_of[7], 71), 0),
        "block_rows": draw_block_rows(jax.random.fold_in(key_of[7], 71), 0),
        "block_cols": draw_block_cols(jax.random.fold_in(key_of[7], 71), 0),
        "block_live": draw_block_live(jax.random.fold_in(key_of[7], 71), 0),
    }


def reference(features, weight, cotangent, adj_values, block_rows, block_cols, block_live):
    block_total = OWNER_ROW_BLOCKS * N_ROW
    device_total = N_ROW * N_REP
    owner_ids = jnp.arange(device_total, dtype=jnp.int32) // N_REP
    row_index = (owner_ids[:, None] * OWNER_ROW_BLOCKS + block_rows.reshape(device_total, KB).astype(jnp.int32)).astype(jnp.int32)
    col_index = block_cols.reshape(device_total, KB).astype(jnp.int32)
    alive_mask = block_live.reshape(device_total, KB).astype(jnp.float32)
    tile_values = adj_values.reshape(device_total, KB, TILE, TILE)
    feature_blocks = features.astype(jnp.float32).reshape(block_total, TILE, D_IN)

    def forward_step(running, slices):
        tiles_now, rows_now, cols_now, alive_now = slices
        products = jnp.einsum("kij,kjf->kif", tiles_now.astype(jnp.float32), feature_blocks[cols_now], precision=lax.Precision.HIGHEST)
        return running.at[rows_now].add(products * alive_now[:, None, None]), None

    start_zero = jnp.zeros((block_total, TILE, D_IN), jnp.float32)
    summed, _ = lax.scan(forward_step, start_zero, (tile_values, row_index, col_index, alive_mask))
    aggregated = summed.reshape(NODES, D_IN).astype(jnp.bfloat16)
    out_rows = jnp.dot(aggregated, weight, preferred_element_type=jnp.float32).astype(jnp.bfloat16)
    grad_weight = jnp.dot(aggregated.T, cotangent, preferred_element_type=jnp.float32) * (NODES ** -0.5)
    projected = jnp.dot(cotangent, weight.T, preferred_element_type=jnp.float32).astype(jnp.bfloat16)
    projected_blocks = projected.astype(jnp.float32).reshape(block_total, TILE, D_IN)

    def backward_step(running, slices):
        tiles_now, rows_now, cols_now, alive_now = slices
        products = jnp.einsum("kji,kjf->kif", tiles_now.astype(jnp.float32), projected_blocks[rows_now], precision=lax.Precision.HIGHEST)
        return running.at[cols_now].add(products * alive_now[:, None, None]), None

    back_sum, _ = lax.scan(backward_step, start_zero, (tile_values, row_index, col_index, alive_mask))
    grad_features = back_sum.reshape(NODES, D_IN).astype(jnp.bfloat16)
    return (out_rows, grad_weight, grad_features)
```

```python
import functools

import jax
import jax.numpy as jnp
from jax import lax
from jax.experimental import pallas as pl
from jax.experimental.pallas import tpu as pltpu
from jax.sharding import Mesh
from jax.sharding import PartitionSpec as P

BF16 = jnp.bfloat16
F32 = jnp.float32
GROUP = 8
QUARTERS = 4
LIMIT = 40 * 1024 * 1024


def vmem_call(kernel, out_shape, in_specs, scratch=()):
    return pl.pallas_call(
        kernel,
        out_shape=out_shape,
        in_specs=in_specs,
        out_specs=jax.tree.map(lambda _: pl.BlockSpec(memory_space=pltpu.VMEM), out_shape),
        scratch_shapes=scratch,
        compiler_params=pltpu.CompilerParams(vmem_limit_bytes=LIMIT),
    )


VMEM = pl.BlockSpec(memory_space=pltpu.VMEM)
SMEM = pl.BlockSpec(memory_space=pltpu.SMEM)
ANY = pl.BlockSpec(memory_space=pl.ANY)


def split_wide(wide):
    half = wide.shape[1] // 2
    return jnp.concatenate([wide[:, :half], wide[:, half:]], axis=0)


def two_words(total):
    high = total.astype(BF16)
    low = (total - high.astype(F32)).astype(BF16)
    return jnp.concatenate([high, low], axis=0)


def source_kernel(pos, features, cotangent, weight, out):
    tile = out.shape[1]
    rows = pl.ds(pl.multiple_of(pos[0] * tile, tile), tile)
    projected = lax.dot_general(
        cotangent[rows, :], weight[...], (((1,), (1,)), ((), ())), preferred_element_type=F32
    ).astype(BF16)
    kept = jnp.where(pos[1] == 0, features[rows, :].astype(F32), projected.astype(F32)).astype(BF16)
    out[...] = jnp.broadcast_to(kept[None], out.shape)


def tile_kernel(
    pos, own_index, mate_index, own_tiles, mate_tiles, x_own, x_next, x_far_a, x_far_b, x_prev,
    cotangent, out, tiles, blocks, total, tile_list, block_list, counts, sems,
):
    slots = own_tiles.shape[0]
    owners = x_own.shape[0]
    tile = own_tiles.shape[1]
    stride = tile_list.shape[0] // QUARTERS
    zero_block = QUARTERS * owners
    copies = []
    at = 0
    for source in (own_tiles, mate_tiles):
        copies.append((source, tiles.at[pl.ds(at, slots)]))
        at += slots
    at = 0
    for source in (x_own, x_next, x_far_a, x_far_b, x_prev):
        copies.append((source, blocks.at[pl.ds(at, source.shape[0])]))
        at += source.shape[0]
    copies = [
        pltpu.make_async_copy(source, target, sems.at[i])
        for i, (source, target) in enumerate(copies)
    ]
    for copy in copies:
        copy.start()
    blocks[zero_block] = jnp.zeros(blocks.shape[1:], BF16)
    total[...] = jnp.zeros_like(total)
    for r in range(QUARTERS):
        counts[r] = 0
    quarter = pos[0]
    for first, index in ((0, own_index), (slots, mate_index)):

        def place(s, carry, first=first, index=index):
            r = index[0, s]
            col = index[1, s]
            n = counts[r]
            tile_list[r * stride + n] = first + s
            block_list[r * stride + n] = ((col - quarter) & 3) * owners + (col >> 2)
            counts[r] = n + index[2, s]
            return carry

        lax.fori_loop(0, slots, place, 0, unroll=8)
    for r in range(QUARTERS):
        for j in range(GROUP):
            tile_list[r * stride + counts[r] + j] = 0
            block_list[r * stride + counts[r] + j] = zero_block
    for copy in copies:
        copy.wait()
    for r in range(QUARTERS):

        def step(g, carry, r=r):
            base = r * stride + g * GROUP
            left = jnp.concatenate(
                [tiles[tile_list[base + j]] for j in range(GROUP)], axis=1
            )
            right = jnp.concatenate(
                [blocks[block_list[base + j]] for j in range(GROUP)], axis=0
            )
            total[r] += jnp.dot(left, right, preferred_element_type=F32)
            return carry

        lax.fori_loop(0, (counts[r] + GROUP - 1) >> 3, step, 0)
    rounded = total[...].astype(BF16)
    grad = lax.dot_general(
        rounded.reshape(QUARTERS * tile, tile),
        cotangent[...],
        (((0,), (0,)), ((), ())),
        preferred_element_type=F32,
    )
    part = grad.shape[0] // QUARTERS
    for q in range(QUARTERS):
        out[q, :tile] = rounded[q]
        out[q, tile:] = two_words(split_wide(grad[q * part : (q + 1) * part]))


def pair_sum(total):
    half = total.shape[0] // 2
    return total[:half] + total[half:]


def member_kernel(got, out):
    tile = got.shape[2]
    total = jnp.sum(got[...].astype(F32), axis=0)
    packed = jnp.concatenate(
        [total[:tile].astype(BF16), two_words(pair_sum(total[tile:]))], axis=0
    )
    out[...] = jnp.broadcast_to(packed[None], out.shape)


def final_kernel(got, rows_out, out):
    tile = got.shape[2]
    total = jnp.sum(got[...].astype(F32), axis=0)
    rows_out[...] = total[:tile].astype(BF16)
    out[...] = jnp.broadcast_to(two_words(pair_sum(total[tile:]))[None], out.shape)


def grad_kernel(scale, got, rows, out):
    tile = rows.shape[0]
    total = pair_sum(jnp.sum(got[...].astype(F32), axis=0)) * scale
    packed = jnp.concatenate([rows[...], two_words(total)], axis=0)
    out[...] = jnp.broadcast_to(packed[None], out.shape)


def output_kernel(got, weight, out_rows, grad_weight, grad_features):
    tile = got.shape[2]
    for q in range(QUARTERS):
        rows = slice(q * tile, (q + 1) * tile)
        out_rows[rows] = jnp.dot(
            got[2 * q, :tile], weight[...], preferred_element_type=F32
        ).astype(BF16)
        grad_features[rows] = got[2 * q + 1, :tile]
        words = pair_sum(got[2 * q, tile:].astype(F32))
        part = words.shape[0] // 2
        grad_weight[q * part : (q + 1) * part] = jnp.concatenate(
            [words[:part], words[part:]], axis=1
        )


def to_all(value, axis):
    return lax.all_to_all(value, axis, 0, 0, tiled=True)


def local(features, weight, cotangent, adj_values, block_rows, block_cols, block_live):
    owners = lax.axis_size("row")
    hi = lax.axis_size("hi")
    quarters = lax.axis_size("x")
    slots, tile = adj_values.shape[:2]
    width = weight.shape[1]
    nodes = features.shape[0] * owners
    ring = lambda step: [(i, (i + step) % quarters) for i in range(quarters)]
    swap = [(0, 1), (1, 0)]
    part = weight.shape[0] // QUARTERS
    tail = 2 * part * (width // tile)

    pos = jnp.stack([lax.axis_index("x"), lax.axis_index("core")]).astype(jnp.int32)
    mate_tiles = lax.ppermute(adj_values, "core", swap)
    own_index = jnp.stack([block_rows, block_cols, block_live])
    mate_index = lax.ppermute(own_index, "core", swap)

    source = vmem_call(
        source_kernel,
        jax.ShapeDtypeStruct((owners, tile, tile), BF16),
        [SMEM, VMEM, VMEM, VMEM],
    )(pos, features, cotangent, weight)
    x_own = to_all(source, "row")
    x_prev = lax.ppermute(x_own, "x", ring(1))
    x_next = lax.ppermute(x_own, "x", ring(-1))
    half = owners // 2
    x_far_a = lax.ppermute(x_prev[:half], "x", ring(1))
    x_far_b = lax.ppermute(x_next[half:], "x", ring(-1))

    stride = 2 * slots + 2 * GROUP
    partial = vmem_call(
        tile_kernel,
        jax.ShapeDtypeStruct((QUARTERS, tile + tail, tile), BF16),
        [SMEM, SMEM, SMEM] + [ANY] * 7 + [VMEM],
        [
            pltpu.VMEM((2 * slots, tile, tile), BF16),
            pltpu.VMEM((QUARTERS * owners + 1, tile, tile), BF16),
            pltpu.VMEM((QUARTERS, tile, tile), F32),
            pltpu.SMEM((QUARTERS * stride,), jnp.int32),
            pltpu.SMEM((QUARTERS * stride,), jnp.int32),
            pltpu.SMEM((QUARTERS,), jnp.int32),
            pltpu.SemaphoreType.DMA((7,)),
        ],
    )(
        pos, own_index, mate_index, adj_values, mate_tiles,
        x_own, x_next, x_far_a, x_far_b, x_prev, cotangent,
    )

    got = to_all(partial, "x")
    got = to_all(
        vmem_call(
            member_kernel, jax.ShapeDtypeStruct((hi, tile + tail, tile), BF16), [VMEM]
        )(got),
        "hi",
    )
    rows, terms = vmem_call(
        final_kernel,
        (
            jax.ShapeDtypeStruct((tile, tile), BF16),
            jax.ShapeDtypeStruct((owners, tail, tile), BF16),
        ),
        [VMEM],
    )(got)
    terms = to_all(terms, "row")
    packed = vmem_call(
        functools.partial(grad_kernel, nodes ** (-0.5)),
        jax.ShapeDtypeStruct((2 * quarters, tile + tail, tile), BF16),
        [VMEM, VMEM],
    )(terms, rows)
    got = to_all(packed, ("x", "core"))
    return vmem_call(
        output_kernel,
        (
            jax.ShapeDtypeStruct((features.shape[0], width), BF16),
            jax.ShapeDtypeStruct(weight.shape, F32),
            jax.ShapeDtypeStruct(features.shape, BF16),
        ),
        [VMEM, VMEM],
    )(got, weight)


def solution(mesh):
    owners, members = mesh.devices.shape
    fine = Mesh(
        mesh.devices.reshape(owners, members // (2 * QUARTERS), QUARTERS, 2),
        ("row", "hi", "x", "core"),
    )
    tiles = ("row", "hi", "x", "core")
    in_specs = (
        P("row", None),
        P(),
        P("row", None),
        P(tiles, None, None),
        P(tiles),
        P(tiles),
        P(tiles),
    )
    out_specs = (P("row", None), P(), P("row", None))
    return jax.shard_map(local, mesh=fine, in_specs=in_specs, out_specs=out_specs, check_vma=False)
```

```python
import functools

import jax
import jax.numpy as jnp
from jax import lax
from jax.experimental import pallas as pl
from jax.experimental.pallas import tpu as pltpu
from jax.sharding import Mesh
from jax.sharding import PartitionSpec as P

BF16 = jnp.bfloat16
F32 = jnp.float32
GROUP = 8
QUARTERS = 4
LIMIT = 12 * 1024 * 1024
SMALL = 1024 * 1024
SEGMENTS = 5
VMEM = pl.BlockSpec(memory_space=pltpu.VMEM)
SMEM = pl.BlockSpec(memory_space=pltpu.SMEM)
ANY = pl.BlockSpec(memory_space=pl.ANY)


def kernel_call(kernel, out_shape, in_specs, out_specs=None, scratch=()):
    if out_specs is None:
        out_specs = jax.tree.map(lambda _: VMEM, out_shape)
    return pl.pallas_call(
        kernel,
        out_shape=out_shape,
        in_specs=in_specs,
        out_specs=out_specs,
        scratch_shapes=scratch,
        compiler_params=pltpu.CompilerParams(vmem_limit_bytes=LIMIT),
    )


def split_wide(wide):
    half = wide.shape[1] // 2
    return jnp.concatenate([wide[:, :half], wide[:, half:]], axis=0)


def two_words(total):
    high = total.astype(BF16)
    low = (total - high.astype(F32)).astype(BF16)
    return jnp.concatenate([high, low], axis=0)


def source_kernel(pos, features, cotangent, weight, out, own_rows, own_terms, factors, sems):
    tile = out.shape[1]
    rows = pl.ds(pl.multiple_of(pos[0] * tile, tile), tile)
    copies = [
        pltpu.make_async_copy(source, target, sems.at[i])
        for i, (source, target) in enumerate(
            (
                (features.at[rows, :], own_rows),
                (cotangent.at[rows, :], own_terms),
                (weight, factors),
            )
        )
    ]
    for copy in copies:
        copy.start()
    for copy in copies:
        copy.wait()
    projected = lax.dot_general(
        own_terms[...], factors[...], (((1,), (1,)), ((), ())), preferred_element_type=F32
    ).astype(BF16)
    kept = jnp.where(pos[1] == 0, own_rows[...].astype(F32), projected.astype(F32)).astype(BF16)
    out[...] = jnp.broadcast_to(kept[None], out.shape)


def multiply(segment, group, tiles, blocks, lists, counts, total):
    stride = lists.shape[0] // (SEGMENTS * QUARTERS)
    for r in range(QUARTERS):
        place = segment * QUARTERS + r

        def step(g, carry, r=r, place=place):
            words = [lists[place * stride + g * group + j] for j in range(group)]
            left = jnp.concatenate([tiles[word & 1023] for word in words], axis=1)
            right = jnp.concatenate([blocks[word >> 10] for word in words], axis=0)
            total[r] += jnp.dot(left, right, preferred_element_type=F32)
            return carry

        lax.fori_loop(0, lax.div(counts[place] + (group - 1), group), step, 0)


def first_kernel(
    pos, own_index, mate_index, own_tiles, mate_tiles, x_own, tiles, lists, counts, total, sems
):
    slots = own_tiles.shape[0]
    half = x_own.shape[0] // 2
    stride = lists.shape[0] // (SEGMENTS * QUARTERS)
    copies = [
        pltpu.make_async_copy(source, tiles.at[pl.ds(i * slots, slots)], sems.at[i])
        for i, source in enumerate((own_tiles, mate_tiles))
    ]
    for copy in copies:
        copy.start()
    tiles[2 * slots] = jnp.zeros(tiles.shape[1:], BF16)
    total[...] = jnp.zeros_like(total)
    for place in range(SEGMENTS * QUARTERS):
        counts[place] = 0
    quarter = pos[0]
    for first, index in ((0, own_index), (slots, mate_index)):

        def put(s, carry, first=first, index=index):
            col = index[1, s]
            turn = (col - quarter) & 3
            owner = col >> 2
            late = (owner >= half).astype(jnp.int32) * (turn == 2).astype(jnp.int32)
            segment = turn + jnp.where(turn == 3, 1, late)
            place = segment * QUARTERS + index[0, s]
            n = counts[place]
            lists[place * stride + n] = first + s + ((owner - late * half) << 10)
            counts[place] = n + index[2, s]
            return carry

        lax.fori_loop(0, slots, put, 0, unroll=8)
    for place in range(SEGMENTS * QUARTERS):
        n = counts[place]
        for j in range(GROUP):
            lists[place * stride + n + j] = 2 * slots
    for copy in copies:
        copy.wait()
    multiply(0, GROUP, tiles, x_own, lists, counts, total)


def second_kernel(lists, counts, tiles, x_next, x_prev, before, total):
    total[...] = before[...]
    multiply(1, GROUP, tiles, x_next, lists, counts, total)
    multiply(4, GROUP, tiles, x_prev, lists, counts, total)


def third_kernel(
    lists, counts, tiles, x_far_a, x_far_b, before, cotangent, out, total, terms, sem
):
    copy = pltpu.make_async_copy(cotangent, terms, sem)
    copy.start()
    total[...] = before[...]
    multiply(2, GROUP // 2, tiles, x_far_a, lists, counts, total)
    multiply(3, GROUP // 2, tiles, x_far_b, lists, counts, total)
    copy.wait()
    members, _, tile = out.shape
    rounded = total[...].astype(BF16).reshape(QUARTERS * tile, tile)
    grad = lax.dot_general(
        rounded, terms[...], (((0,), (0,)), ((), ())), preferred_element_type=F32
    )
    rows = rounded.shape[0] // members
    part = grad.shape[0] // members
    for m in range(members):
        out[m, :rows] = rounded[m * rows : (m + 1) * rows]
        out[m, rows:] = two_words(split_wide(grad[m * part : (m + 1) * part]))


def pair_sum(total):
    half = total.shape[0] // 2
    return total[:half] + total[half:]


def member_kernel(got, rows_out, out):
    rows = rows_out.shape[0]
    total = jnp.sum(got[...].astype(F32), axis=0)
    rows_out[...] = total[:rows].astype(BF16)
    out[...] = jnp.broadcast_to(two_words(pair_sum(total[rows:]))[None], out.shape)


def grad_kernel(scale, got, rows, out):
    total = pair_sum(jnp.sum(got[...].astype(F32), axis=0)) * scale
    packed = jnp.concatenate([rows[...], two_words(total)], axis=0)
    out[...] = jnp.broadcast_to(packed[None], out.shape)


def output_kernel(pos, mine, mate, weight, out_rows, grad_weight, grad_features):
    members, packet, tile = mine.shape
    rows = out_rows.shape[0] // members
    part = grad_weight.shape[0] // members

    def write(forward, backward):
        for m in range(members):
            grad_features[m * rows : (m + 1) * rows] = backward[m, :rows]
            words = pair_sum(forward[m, rows:].astype(F32))
            grad_weight[m * part : (m + 1) * part] = jnp.concatenate(
                [words[:part], words[part:]], axis=1
            )
        aggregated = forward[:, :rows].reshape(members * rows, tile)
        out_rows[...] = jnp.dot(
            aggregated, weight[...], preferred_element_type=F32
        ).astype(BF16)

    pl.when(pos[1] == 0)(lambda: write(mine, mate))
    pl.when(pos[1] == 1)(lambda: write(mate, mine))


def after(value, other):
    return pl.pallas_call(
        lambda *refs: None,
        out_shape=jax.ShapeDtypeStruct(value.shape, value.dtype),
        in_specs=[ANY, ANY],
        out_specs=ANY,
        input_output_aliases={0: 0},
        compiler_params=pltpu.CompilerParams(vmem_limit_bytes=SMALL),
    )(value, other)


def in_hbm(value):
    return pltpu.with_memory_space_constraint(value, pltpu.HBM)


def to_all(value, axis):
    return lax.all_to_all(value, axis, 0, 0, tiled=True)


def local(features, weight, cotangent, adj_values, block_rows, block_cols, block_live):
    owners = lax.axis_size("row")
    quarters = lax.axis_size("x")
    members = lax.axis_size("hi") * quarters
    slots, tile = adj_values.shape[:2]
    width = weight.shape[1]
    nodes = features.shape[0] * owners
    ring = lambda step: [(i, (i + step) % quarters) for i in range(quarters)]
    swap = [(0, 1), (1, 0)]
    rows = features.shape[0] // members
    tail = 2 * (weight.shape[0] // members) * (width // tile)
    packet = jax.ShapeDtypeStruct((members, rows + tail, tile), BF16)

    pos = jnp.stack([lax.axis_index("x"), lax.axis_index("core")]).astype(jnp.int32)
    own_index = jnp.stack([block_rows, block_cols, block_live])
    mate_index = lax.ppermute(own_index, "core", swap)
    mate_tiles = lax.ppermute(adj_values, "core", swap)

    source = kernel_call(
        source_kernel,
        jax.ShapeDtypeStruct((owners, tile, tile), BF16),
        [SMEM, ANY, ANY, ANY],
        scratch=[
            pltpu.VMEM((tile, tile), BF16),
            pltpu.VMEM((tile, width), BF16),
            pltpu.VMEM(weight.shape, BF16),
            pltpu.SemaphoreType.DMA((3,)),
        ],
    )(pos, in_hbm(features), in_hbm(cotangent), in_hbm(weight))
    x_own = after(to_all(source, "row"), mate_index)
    x_prev = lax.ppermute(x_own, "x", ring(1))
    x_next = lax.ppermute(x_own, "x", ring(-1))

    places = SEGMENTS * QUARTERS
    sums = jax.ShapeDtypeStruct((QUARTERS, tile, tile), F32)
    tiles, lists, counts, total = kernel_call(
        first_kernel,
        (
            jax.ShapeDtypeStruct((2 * slots + 1, tile, tile), BF16),
            jax.ShapeDtypeStruct((places * (2 * slots + GROUP),), jnp.int32),
            jax.ShapeDtypeStruct((places,), jnp.int32),
            sums,
        ),
        [SMEM, SMEM, SMEM, ANY, ANY, VMEM],
        out_specs=(VMEM, SMEM, SMEM, VMEM),
        scratch=[pltpu.SemaphoreType.DMA((2,))],
    )(pos, own_index, mate_index, in_hbm(adj_values), mate_tiles, x_own)

    half = owners // 2
    x_prev, x_next = after(x_prev, counts), after(x_next, counts)
    x_far_a = lax.ppermute(x_prev[:half], "x", ring(1))
    x_far_b = lax.ppermute(x_next[half:], "x", ring(-1))
    total = kernel_call(second_kernel, sums, [SMEM, SMEM] + [VMEM] * 4)(
        lists, counts, tiles, x_next, x_prev, total
    )
    partial = kernel_call(
        third_kernel,
        packet,
        [SMEM, SMEM] + [VMEM] * 4 + [ANY],
        scratch=[
            pltpu.VMEM((QUARTERS, tile, tile), F32),
            pltpu.VMEM(cotangent.shape, BF16),
            pltpu.SemaphoreType.DMA,
        ],
    )(lists, counts, tiles, x_far_a, x_far_b, total, in_hbm(cotangent))

    got = to_all(partial, ("hi", "x"))
    done, terms = kernel_call(
        member_kernel,
        (
            jax.ShapeDtypeStruct((rows, tile), BF16),
            jax.ShapeDtypeStruct((owners, tail, tile), BF16),
        ),
        [VMEM],
    )(got)
    terms = to_all(terms, "row")
    packed = kernel_call(
        functools.partial(grad_kernel, nodes ** (-0.5)), packet, [VMEM, VMEM]
    )(terms, done)
    mine = to_all(packed, ("hi", "x"))
    mate = lax.ppermute(mine, "core", swap)
    return kernel_call(
        output_kernel,
        (
            jax.ShapeDtypeStruct((features.shape[0], width), BF16),
            jax.ShapeDtypeStruct(weight.shape, F32),
            jax.ShapeDtypeStruct(features.shape, BF16),
        ),
        [SMEM, VMEM, VMEM, VMEM],
    )(pos, mine, mate, weight)


def solution(mesh):
    owners, members = mesh.devices.shape
    fine = Mesh(
        mesh.devices.reshape(owners, members // (2 * QUARTERS), QUARTERS, 2),
        ("row", "hi", "x", "core"),
    )
    tiles = ("row", "hi", "x", "core")
    in_specs = (
        P("row", None),
        P(),
        P("row", None),
        P(tiles, None, None),
        P(tiles),
        P(tiles),
        P(tiles),
    )
    out_specs = (P("row", None), P(), P("row", None))
    return jax.shard_map(local, mesh=fine, in_specs=in_specs, out_specs=out_specs, check_vma=False)
```

```python
import functools

import jax
import jax.numpy as jnp
from jax import lax
from jax.experimental import pallas as pl
from jax.experimental.pallas import tpu as pltpu
from jax.sharding import Mesh
from jax.sharding import PartitionSpec as P

BF16 = jnp.bfloat16
F32 = jnp.float32
GROUP = 8
QUARTERS = 4
LIMIT = 12 * 1024 * 1024
SEGMENTS = 3
VMEM = pl.BlockSpec(memory_space=pltpu.VMEM)
SMEM = pl.BlockSpec(memory_space=pltpu.SMEM)
ANY = pl.BlockSpec(memory_space=pl.ANY)


def kernel_call(kernel, out_shape, in_specs, out_specs=None, scratch=()):
    if out_specs is None:
        out_specs = jax.tree.map(lambda _: VMEM, out_shape)
    return pl.pallas_call(
        kernel,
        out_shape=out_shape,
        in_specs=in_specs,
        out_specs=out_specs,
        scratch_shapes=scratch,
        compiler_params=pltpu.CompilerParams(vmem_limit_bytes=LIMIT),
    )


def split_wide(wide):
    half = wide.shape[1] // 2
    return jnp.concatenate([wide[:, :half], wide[:, half:]], axis=0)


def source_kernel(pos, features, cotangent, weight, out, own_rows, own_terms, factors, sems):
    tile = out.shape[1]
    rows = pl.ds(pl.multiple_of(pos[0] * tile, tile), tile)
    copies = [
        pltpu.make_async_copy(source, target, sems.at[i])
        for i, (source, target) in enumerate(
            (
                (features.at[rows, :], own_rows),
                (cotangent.at[rows, :], own_terms),
                (weight, factors),
            )
        )
    ]
    for copy in copies:
        copy.start()
    for copy in copies:
        copy.wait()
    projected = lax.dot_general(
        own_terms[...], factors[...], (((1,), (1,)), ((), ())), preferred_element_type=F32
    ).astype(BF16)
    kept = jnp.where(pos[1] == 0, own_rows[...].astype(F32), projected.astype(F32)).astype(BF16)
    out[...] = jnp.broadcast_to(kept[None], out.shape)


def multiply(segment, tiles, blocks, lists, counts, total):
    stride = lists.shape[0] // (SEGMENTS * QUARTERS)
    longest = counts[segment * QUARTERS]
    for r in range(1, QUARTERS):
        longest = jnp.maximum(longest, counts[segment * QUARTERS + r])

    def step(g, carry):
        for r in range(QUARTERS):
            at = (segment * QUARTERS + r) * stride + g * GROUP
            words = [lists[at + j] for j in range(GROUP)]
            left = jnp.concatenate([tiles[word & 1023] for word in words], axis=1)
            right = jnp.concatenate([blocks[word >> 10] for word in words], axis=0)
            total[r] += jnp.dot(left, right, preferred_element_type=F32)
        return carry

    lax.fori_loop(0, (longest + (GROUP - 1)) >> 3, step, 0)


def collect(parts, whole, sems):
    copies = []
    at = 0
    for i, part in enumerate(parts):
        copies.append(
            pltpu.make_async_copy(part, whole.at[pl.ds(at, part.shape[0])], sems.at[i])
        )
        at += part.shape[0]
    for copy in copies:
        copy.start()
    return copies


def list_kernel(
    owners, pos, own_index, mate_index, own_tiles, mate_tiles, tiles, lists, counts, sems
):
    slots = own_tiles.shape[0]
    stride = lists.shape[0] // (SEGMENTS * QUARTERS)
    copies = collect((own_tiles, mate_tiles), tiles, sems)
    tiles[2 * slots] = jnp.zeros(tiles.shape[1:], BF16)
    for place in range(SEGMENTS * QUARTERS):
        counts[place] = 0

    def clear(i, carry):
        lists[i] = 2 * slots
        return carry

    lax.fori_loop(0, lists.shape[0], clear, 0, unroll=16)
    quarter = pos[0]
    for first, index in ((0, own_index), (slots, mate_index)):

        def put(s, carry, first=first, index=index):
            col = index[1, s]
            turn = (col - quarter) & 3
            segment = jnp.where(turn == 3, 1, turn)
            block = (col >> 2) + jnp.where(turn == 3, owners, 0)
            place = segment * QUARTERS + index[0, s]
            n = counts[place]
            lists[place * stride + n] = first + s + (block << 10)
            counts[place] = n + index[2, s]
            return carry

        lax.fori_loop(0, slots, put, 0, unroll=8)
    for place in range(SEGMENTS * QUARTERS):
        lists[place * stride + counts[place]] = 2 * slots
    for copy in copies:
        copy.wait()


def halves_kernel(x_own, counts, low, high):
    half = low.shape[0]
    low[...] = x_own[:half]
    high[...] = x_own[half:]


def own_kernel(lists, counts, tiles, x_own, total):
    total[...] = jnp.zeros_like(total)
    multiply(0, tiles, x_own, lists, counts, total)


def near_kernel(lists, counts, tiles, next_a, next_b, prev_a, prev_b, before, total, blocks, sems):
    copies = collect((next_a, next_b, prev_a, prev_b), blocks, sems)
    total[...] = before[...]
    for copy in copies:
        copy.wait()
    multiply(1, tiles, blocks, lists, counts, total)


def far_kernel(
    lists, counts, tiles, far_a, far_b, before, cotangent, out, total, blocks, terms, sems
):
    copies = collect((far_a, far_b), blocks, sems)
    load = pltpu.make_async_copy(cotangent, terms, sems.at[2])
    load.start()
    total[...] = before[...]
    for copy in copies:
        copy.wait()
    multiply(2, tiles, blocks, lists, counts, total)
    load.wait()
    members, _, tile = out.shape
    rounded = total[...].astype(BF16).reshape(QUARTERS * tile, tile)
    grad = lax.dot_general(
        rounded, terms[...], (((0,), (0,)), ((), ())), preferred_element_type=F32
    )
    rows = rounded.shape[0] // members
    part = grad.shape[0] // members
    for m in range(members):
        out[m, :rows] = rounded[m * rows : (m + 1) * rows]
        out[m, rows:] = split_wide(grad[m * part : (m + 1) * part]).astype(BF16)


def member_kernel(got, rows_out, out):
    rows = rows_out.shape[0]
    total = jnp.sum(got[...].astype(F32), axis=0).astype(BF16)
    rows_out[...] = total[:rows]
    out[...] = jnp.broadcast_to(total[rows:][None], out.shape)


def grad_kernel(scale, got, rows, out):
    total = jnp.sum(got[...].astype(F32), axis=0) * scale
    packed = jnp.concatenate([rows[...], total.astype(BF16)], axis=0)
    out[...] = jnp.broadcast_to(packed[None], out.shape)


def output_kernel(pos, mine, mate, weight, out_rows, grad_weight, grad_features):
    members, packet, tile = mine.shape
    rows = out_rows.shape[0] // members
    part = grad_weight.shape[0] // members

    def write(forward, backward):
        for m in range(members):
            grad_features[m * rows : (m + 1) * rows] = backward[m, :rows]
            words = forward[m, rows:].astype(F32)
            grad_weight[m * part : (m + 1) * part] = jnp.concatenate(
                [words[:part], words[part:]], axis=1
            )
        aggregated = forward[:, :rows].reshape(members * rows, tile)
        out_rows[...] = jnp.dot(
            aggregated, weight[...], preferred_element_type=F32
        ).astype(BF16)

    pl.when(pos[1] == 0)(lambda: write(mine, mate))
    pl.when(pos[1] == 1)(lambda: write(mate, mine))


def in_hbm(value):
    return pltpu.with_memory_space_constraint(value, pltpu.HBM)


def to_all(value, axis):
    return lax.all_to_all(value, axis, 0, 0, tiled=True)


def local(features, weight, cotangent, adj_values, block_rows, block_cols, block_live):
    owners = lax.axis_size("row")
    quarters = lax.axis_size("x")
    members = lax.axis_size("hi") * quarters
    slots, tile = adj_values.shape[:2]
    width = weight.shape[1]
    nodes = features.shape[0] * owners
    ring = lambda step: [(i, (i + step) % quarters) for i in range(quarters)]
    swap = [(0, 1), (1, 0)]
    rows = features.shape[0] // members
    tail = (weight.shape[0] // members) * (width // tile)
    packet = jax.ShapeDtypeStruct((members, rows + tail, tile), BF16)

    pos = jnp.stack([lax.axis_index("x"), lax.axis_index("core")]).astype(jnp.int32)
    own_index = jnp.stack([block_rows, block_cols, block_live])
    mate_index = lax.ppermute(own_index, "core", swap)

    source = kernel_call(
        source_kernel,
        jax.ShapeDtypeStruct((owners, tile, tile), BF16),
        [SMEM, ANY, ANY, ANY],
        scratch=[
            pltpu.VMEM((tile, tile), BF16),
            pltpu.VMEM((tile, width), BF16),
            pltpu.VMEM(weight.shape, BF16),
            pltpu.SemaphoreType.DMA((3,)),
        ],
    )(pos, in_hbm(features), in_hbm(cotangent), in_hbm(weight))
    own_tiles, source = lax.optimization_barrier((adj_values, source))
    mate_tiles = lax.ppermute(own_tiles, "core", swap)
    places = SEGMENTS * QUARTERS
    sums = jax.ShapeDtypeStruct((QUARTERS, tile, tile), F32)
    tiles, lists, counts = kernel_call(
        functools.partial(list_kernel, owners),
        (
            jax.ShapeDtypeStruct((2 * slots + 1, tile, tile), BF16),
            jax.ShapeDtypeStruct((places * (2 * slots + GROUP),), jnp.int32),
            jax.ShapeDtypeStruct((places,), jnp.int32),
        ),
        [SMEM, SMEM, SMEM, ANY, ANY],
        out_specs=(VMEM, SMEM, SMEM),
        scratch=[pltpu.SemaphoreType.DMA((2,))],
    )(pos, own_index, mate_index, in_hbm(adj_values), mate_tiles)
    x_own = to_all(source, "row")

    part = jax.ShapeDtypeStruct((owners // 2, tile, tile), BF16)
    low, high = kernel_call(halves_kernel, (part, part), [VMEM, SMEM])(x_own, counts)
    prev_a = lax.ppermute(low, "x", ring(1))
    next_b = lax.ppermute(high, "x", ring(-1))
    prev_b = lax.ppermute(high, "x", ring(1))
    next_a = lax.ppermute(low, "x", ring(-1))
    far_a = lax.ppermute(prev_a, "x", ring(1))
    far_b = lax.ppermute(next_b, "x", ring(-1))
    total = kernel_call(own_kernel, sums, [SMEM, SMEM, VMEM, VMEM])(lists, counts, tiles, x_own)
    total = kernel_call(
        near_kernel,
        sums,
        [SMEM, SMEM] + [VMEM] * 6,
        scratch=[
            pltpu.VMEM((2 * owners, tile, tile), BF16),
            pltpu.SemaphoreType.DMA((4,)),
        ],
    )(lists, counts, tiles, next_a, next_b, prev_a, prev_b, total)
    partial = kernel_call(
        far_kernel,
        packet,
        [SMEM, SMEM] + [VMEM] * 4 + [ANY],
        scratch=[
            pltpu.VMEM((QUARTERS, tile, tile), F32),
            pltpu.VMEM((owners, tile, tile), BF16),
            pltpu.VMEM(cotangent.shape, BF16),
            pltpu.SemaphoreType.DMA((3,)),
        ],
    )(lists, counts, tiles, far_a, far_b, total, in_hbm(cotangent))

    got = to_all(partial, ("hi", "x"))
    done, terms = kernel_call(
        member_kernel,
        (
            jax.ShapeDtypeStruct((rows, tile), BF16),
            jax.ShapeDtypeStruct((owners, tail, tile), BF16),
        ),
        [VMEM],
    )(got)
    terms = to_all(terms, "row")
    packed = kernel_call(
        functools.partial(grad_kernel, nodes ** (-0.5)), packet, [VMEM, VMEM]
    )(terms, done)
    mine = to_all(packed, ("hi", "x"))
    mate = lax.ppermute(mine, "core", swap)
    return kernel_call(
        output_kernel,
        (
            jax.ShapeDtypeStruct((features.shape[0], width), BF16),
            jax.ShapeDtypeStruct(weight.shape, F32),
            jax.ShapeDtypeStruct(features.shape, BF16),
        ),
        [SMEM, VMEM, VMEM, VMEM],
    )(pos, mine, mate, weight)


def solution(mesh):
    owners, members = mesh.devices.shape
    fine = Mesh(
        mesh.devices.reshape(owners, members // (2 * QUARTERS), QUARTERS, 2),
        ("row", "hi", "x", "core"),
    )
    tiles = ("row", "hi", "x", "core")
    in_specs = (
        P("row", None),
        P(),
        P("row", None),
        P(tiles, None, None),
        P(tiles),
        P(tiles),
        P(tiles),
    )
    out_specs = (P("row", None), P(), P("row", None))
    return jax.shard_map(local, mesh=fine, in_specs=in_specs, out_specs=out_specs, check_vma=False)
```

```python
import functools

import jax
import jax.numpy as jnp
from jax import lax
from jax.experimental import pallas as pl
from jax.experimental.pallas import tpu as pltpu
from jax.sharding import Mesh
from jax.sharding import PartitionSpec as P

BF16 = jnp.bfloat16
F32 = jnp.float32
GROUP = 8
QUARTERS = 4
LIMIT = 12 * 1024 * 1024
SMALL = 1024 * 1024
SEGMENTS = 4
VMEM = pl.BlockSpec(memory_space=pltpu.VMEM)
SMEM = pl.BlockSpec(memory_space=pltpu.SMEM)
ANY = pl.BlockSpec(memory_space=pl.ANY)


def kernel_call(kernel, out_shape, in_specs, out_specs=None, scratch=()):
    if out_specs is None:
        out_specs = jax.tree.map(lambda _: VMEM, out_shape)
    return pl.pallas_call(
        kernel,
        out_shape=out_shape,
        in_specs=in_specs,
        out_specs=out_specs,
        scratch_shapes=scratch,
        compiler_params=pltpu.CompilerParams(vmem_limit_bytes=LIMIT),
    )


def split_wide(wide):
    half = wide.shape[1] // 2
    return jnp.concatenate([wide[:, :half], wide[:, half:]], axis=0)


def source_kernel(pos, features, cotangent, weight, out, own_rows, own_terms, factors, sems):
    tile = out.shape[1]
    rows = pl.ds(pl.multiple_of(pos[0] * tile, tile), tile)
    copies = [
        pltpu.make_async_copy(source, target, sems.at[i])
        for i, (source, target) in enumerate(
            (
                (features.at[rows, :], own_rows),
                (cotangent.at[rows, :], own_terms),
                (weight, factors),
            )
        )
    ]
    for copy in copies:
        copy.start()
    for copy in copies:
        copy.wait()
    projected = lax.dot_general(
        own_terms[...], factors[...], (((1,), (1,)), ((), ())), preferred_element_type=F32
    ).astype(BF16)
    kept = jnp.where(pos[1] == 0, own_rows[...].astype(F32), projected.astype(F32)).astype(BF16)
    out[...] = jnp.broadcast_to(kept[None], out.shape)


def multiply(segment, tiles, blocks, lists, counts, total):
    stride = lists.shape[0] // (SEGMENTS * QUARTERS)
    longest = counts[segment * QUARTERS]
    for r in range(1, QUARTERS):
        longest = jnp.maximum(longest, counts[segment * QUARTERS + r])

    def step(g, carry):
        for r in range(QUARTERS):
            at = (segment * QUARTERS + r) * stride + g * GROUP
            words = [lists[at + j] for j in range(GROUP)]
            left = jnp.concatenate([tiles[word & 1023] for word in words], axis=1)
            right = jnp.concatenate([blocks[word >> 10] for word in words], axis=0)
            total[r] += jnp.dot(left, right, preferred_element_type=F32)
        return carry

    lax.fori_loop(0, (longest + (GROUP - 1)) >> 3, step, 0)


def collect(parts, whole, sems):
    copies = []
    at = 0
    for i, part in enumerate(parts):
        copies.append(
            pltpu.make_async_copy(part, whole.at[pl.ds(at, part.shape[0])], sems.at[i])
        )
        at += part.shape[0]
    for copy in copies:
        copy.start()
    return copies


def list_kernel(slots, owners, pos, own_index, mate_index, lists, counts):
    stride = lists.shape[0] // (SEGMENTS * QUARTERS)
    for place in range(SEGMENTS * QUARTERS):
        counts[place] = 0

    def clear(i, carry):
        lists[i] = 2 * slots
        return carry

    lax.fori_loop(0, lists.shape[0], clear, 0, unroll=16)
    quarter = pos[0]
    for first, index in ((0, own_index), (slots, mate_index)):

        def put(s, carry, first=first, index=index):
            col = index[1, s]
            turn = (col - quarter) & 3
            owner = col >> 2
            late = (owner >= owners // 2).astype(jnp.int32) * (turn == 2).astype(jnp.int32)
            segment = jnp.where(turn == 3, 1, turn + late)
            block = owner + jnp.where(turn == 3, owners, -late * (owners // 2))
            place = segment * QUARTERS + index[0, s]
            n = counts[place]
            lists[place * stride + n] = first + s + (block << 10)
            counts[place] = n + index[2, s]
            return carry

        lax.fori_loop(0, slots, put, 0, unroll=8)
    for place in range(SEGMENTS * QUARTERS):
        lists[place * stride + counts[place]] = 2 * slots


def own_kernel(lists, counts, own_tiles, mate_tiles, x_own, tiles, total, sems):
    copies = collect((own_tiles, mate_tiles), tiles, sems)
    total[...] = jnp.zeros_like(total)
    tiles[tiles.shape[0] - 1] = jnp.zeros(tiles.shape[1:], BF16)
    for copy in copies:
        copy.wait()
    multiply(0, tiles, x_own, lists, counts, total)


def near_kernel(lists, counts, tiles, next_a, next_b, prev_a, prev_b, before, total, blocks, sems):
    copies = collect((next_a, next_b, prev_a, prev_b), blocks, sems)
    total[...] = before[...]
    for copy in copies:
        copy.wait()
    multiply(1, tiles, blocks, lists, counts, total)


def far_kernel(lists, counts, tiles, far_a, before, total):
    total[...] = before[...]
    multiply(2, tiles, far_a, lists, counts, total)


def last_kernel(lists, counts, tiles, far_b, before, cotangent, out, total, terms, sem):
    load = pltpu.make_async_copy(cotangent, terms, sem)
    load.start()
    total[...] = before[...]
    multiply(3, tiles, far_b, lists, counts, total)
    load.wait()
    members, _, tile = out.shape
    rounded = total[...].astype(BF16).reshape(QUARTERS * tile, tile)
    grad = lax.dot_general(
        rounded, terms[...], (((0,), (0,)), ((), ())), preferred_element_type=F32
    )
    rows = rounded.shape[0] // members
    part = grad.shape[0] // members
    for m in range(members):
        out[m, :rows] = rounded[m * rows : (m + 1) * rows]
        out[m, rows:] = split_wide(grad[m * part : (m + 1) * part]).astype(BF16)


def member_kernel(got, rows_out, out):
    rows = rows_out.shape[0]
    total = jnp.sum(got[...].astype(F32), axis=0).astype(BF16)
    rows_out[...] = total[:rows]
    out[...] = jnp.broadcast_to(total[rows:][None], out.shape)


def grad_kernel(scale, got, rows, out):
    total = jnp.sum(got[...].astype(F32), axis=0) * scale
    packed = jnp.concatenate([rows[...], total.astype(BF16)], axis=0)
    out[...] = jnp.broadcast_to(packed[None], out.shape)


def output_kernel(pos, mine, mate, weight, out_rows, grad_weight, grad_features):
    members, packet, tile = mine.shape
    rows = out_rows.shape[0] // members
    part = grad_weight.shape[0] // members

    def write(forward, backward):
        for m in range(members):
            grad_features[m * rows : (m + 1) * rows] = backward[m, :rows]
            words = forward[m, rows:].astype(F32)
            grad_weight[m * part : (m + 1) * part] = jnp.concatenate(
                [words[:part], words[part:]], axis=1
            )
        aggregated = forward[:, :rows].reshape(members * rows, tile)
        out_rows[...] = jnp.dot(
            aggregated, weight[...], preferred_element_type=F32
        ).astype(BF16)

    pl.when(pos[1] == 0)(lambda: write(mine, mate))
    pl.when(pos[1] == 1)(lambda: write(mate, mine))


def after(value, other):
    return pl.pallas_call(
        lambda *refs: None,
        out_shape=jax.ShapeDtypeStruct(value.shape, value.dtype),
        in_specs=[ANY, ANY],
        out_specs=ANY,
        input_output_aliases={0: 0},
        compiler_params=pltpu.CompilerParams(vmem_limit_bytes=SMALL),
    )(value, other)


def in_hbm(value):
    return pltpu.with_memory_space_constraint(value, pltpu.HBM)


def to_all(value, axis):
    return lax.all_to_all(value, axis, 0, 0, tiled=True)


def local(features, weight, cotangent, adj_values, block_rows, block_cols, block_live):
    owners = lax.axis_size("row")
    quarters = lax.axis_size("x")
    members = lax.axis_size("hi") * quarters
    slots, tile = adj_values.shape[:2]
    width = weight.shape[1]
    nodes = features.shape[0] * owners
    ring = lambda step: [(i, (i + step) % quarters) for i in range(quarters)]
    swap = [(0, 1), (1, 0)]
    rows = features.shape[0] // members
    tail = (weight.shape[0] // members) * (width // tile)
    packet = jax.ShapeDtypeStruct((members, rows + tail, tile), BF16)

    pos = jnp.stack([lax.axis_index("x"), lax.axis_index("core")]).astype(jnp.int32)

    source = kernel_call(
        source_kernel,
        jax.ShapeDtypeStruct((owners, tile, tile), BF16),
        [SMEM, ANY, ANY, ANY],
        scratch=[
            pltpu.VMEM((tile, tile), BF16),
            pltpu.VMEM((tile, width), BF16),
            pltpu.VMEM(weight.shape, BF16),
            pltpu.SemaphoreType.DMA((3,)),
        ],
    )(pos, in_hbm(features), in_hbm(cotangent), in_hbm(weight))
    own_tiles, *index, source = lax.optimization_barrier(
        (adj_values, block_rows, block_cols, block_live, source)
    )
    mate_tiles = lax.ppermute(own_tiles, "core", swap)
    own_index = jnp.stack(index)
    mate_index = lax.ppermute(own_index, "core", swap)
    places = SEGMENTS * QUARTERS
    sums = jax.ShapeDtypeStruct((QUARTERS, tile, tile), F32)
    lists, counts = kernel_call(
        functools.partial(list_kernel, slots, owners),
        (
            jax.ShapeDtypeStruct((places * (2 * slots + GROUP),), jnp.int32),
            jax.ShapeDtypeStruct((places,), jnp.int32),
        ),
        [SMEM, SMEM, SMEM],
        out_specs=(SMEM, SMEM),
    )(pos, own_index, mate_index)
    x_own = after(to_all(source, "row"), counts)

    half = owners // 2
    low, high = x_own[:half], x_own[half:]
    prev_a = lax.ppermute(low, "x", ring(1))
    next_b = lax.ppermute(high, "x", ring(-1))
    prev_b = lax.ppermute(high, "x", ring(1))
    next_a = lax.ppermute(low, "x", ring(-1))
    far_a = lax.ppermute(prev_a, "x", ring(1))
    far_b = lax.ppermute(next_b, "x", ring(-1))
    tiles, total = kernel_call(
        own_kernel,
        (jax.ShapeDtypeStruct((2 * slots + 1, tile, tile), BF16), sums),
        [SMEM, SMEM, ANY, ANY, VMEM],
        scratch=[pltpu.SemaphoreType.DMA((2,))],
    )(lists, counts, in_hbm(adj_values), mate_tiles, x_own)
    total = kernel_call(
        near_kernel,
        sums,
        [SMEM, SMEM] + [VMEM] * 6,
        scratch=[
            pltpu.VMEM((2 * owners, tile, tile), BF16),
            pltpu.SemaphoreType.DMA((4,)),
        ],
    )(lists, counts, tiles, next_a, next_b, prev_a, prev_b, total)
    total = kernel_call(far_kernel, sums, [SMEM, SMEM] + [VMEM] * 3)(
        lists, counts, tiles, far_a, total
    )
    partial = kernel_call(
        last_kernel,
        packet,
        [SMEM, SMEM] + [VMEM] * 3 + [ANY],
        scratch=[
            pltpu.VMEM((QUARTERS, tile, tile), F32),
            pltpu.VMEM(cotangent.shape, BF16),
            pltpu.SemaphoreType.DMA,
        ],
    )(lists, counts, tiles, far_b, total, in_hbm(cotangent))

    got = to_all(partial, ("hi", "x"))
    done, terms = kernel_call(
        member_kernel,
        (
            jax.ShapeDtypeStruct((rows, tile), BF16),
            jax.ShapeDtypeStruct((owners, tail, tile), BF16),
        ),
        [VMEM],
    )(got)
    terms = to_all(terms, "row")
    packed = kernel_call(
        functools.partial(grad_kernel, nodes ** (-0.5)), packet, [VMEM, VMEM]
    )(terms, done)
    mine = to_all(packed, ("hi", "x"))
    mate = lax.ppermute(mine, "core", swap)
    return kernel_call(
        output_kernel,
        (
            jax.ShapeDtypeStruct((features.shape[0], width), BF16),
            jax.ShapeDtypeStruct(weight.shape, F32),
            jax.ShapeDtypeStruct(features.shape, BF16),
        ),
        [SMEM, VMEM, VMEM, VMEM],
    )(pos, mine, mate, weight)


def solution(mesh):
    owners, members = mesh.devices.shape
    fine = Mesh(
        mesh.devices.reshape(owners, members // (2 * QUARTERS), QUARTERS, 2),
        ("row", "hi", "x", "core"),
    )
    tiles = ("row", "hi", "x", "core")
    in_specs = (
        P("row", None),
        P(),
        P("row", None),
        P(tiles, None, None),
        P(tiles),
        P(tiles),
        P(tiles),
    )
    out_specs = (P("row", None), P(), P("row", None))
    return jax.shard_map(local, mesh=fine, in_specs=in_specs, out_specs=out_specs, check_vma=False)
```

```python
import functools

import jax
import jax.numpy as jnp
from jax import lax
from jax.experimental import pallas as pl
from jax.experimental.pallas import tpu as pltpu
from jax.sharding import Mesh
from jax.sharding import PartitionSpec as P

BF16 = jnp.bfloat16
F32 = jnp.float32
GROUP = 8
QUARTERS = 4
LIMIT = 12 * 1024 * 1024
SMALL = 1024 * 1024
SEGMENTS = 4
VMEM = pl.BlockSpec(memory_space=pltpu.VMEM)
SMEM = pl.BlockSpec(memory_space=pltpu.SMEM)
ANY = pl.BlockSpec(memory_space=pl.ANY)


def kernel_call(kernel, out_shape, in_specs, out_specs=None, scratch=(), aliases=None):
    if out_specs is None:
        out_specs = jax.tree.map(lambda _: VMEM, out_shape)
    return pl.pallas_call(
        kernel,
        out_shape=out_shape,
        in_specs=in_specs,
        out_specs=out_specs,
        scratch_shapes=scratch,
        input_output_aliases=aliases or {},
        compiler_params=pltpu.CompilerParams(vmem_limit_bytes=LIMIT),
    )


def split_wide(wide):
    half = wide.shape[1] // 2
    return jnp.concatenate([wide[:, :half], wide[:, half:]], axis=0)


def source_kernel(pos, features, cotangent, weight, out, own_rows, own_terms, factors, sems):
    tile = out.shape[1]
    rows = pl.ds(pl.multiple_of(pos[0] * tile, tile), tile)
    copies = [
        pltpu.make_async_copy(source, target, sems.at[i])
        for i, (source, target) in enumerate(
            (
                (features.at[rows, :], own_rows),
                (cotangent.at[rows, :], own_terms),
                (weight, factors),
            )
        )
    ]
    for copy in copies:
        copy.start()
    for copy in copies:
        copy.wait()
    projected = lax.dot_general(
        own_terms[...], factors[...], (((1,), (1,)), ((), ())), preferred_element_type=F32
    ).astype(BF16)
    kept = jnp.where(pos[1] == 0, own_rows[...].astype(F32), projected.astype(F32)).astype(BF16)
    out[...] = jnp.broadcast_to(kept[None], out.shape)


def multiply(segment, tiles, blocks, lists, counts, total):
    stride = lists.shape[0] // (SEGMENTS * QUARTERS)
    longest = counts[segment * QUARTERS]
    for r in range(1, QUARTERS):
        longest = jnp.maximum(longest, counts[segment * QUARTERS + r])

    def step(g, carry):
        for r in range(QUARTERS):
            at = (segment * QUARTERS + r) * stride + g * GROUP
            words = [lists[at + j] for j in range(GROUP)]
            left = jnp.concatenate([tiles[word & 1023] for word in words], axis=1)
            right = jnp.concatenate([blocks[word >> 10] for word in words], axis=0)
            total[r] += jnp.dot(left, right, preferred_element_type=F32)
        return carry

    lax.fori_loop(0, (longest + (GROUP - 1)) >> 3, step, 0)


def collect(parts, whole, sems):
    copies = []
    at = 0
    for i, part in enumerate(parts):
        copies.append(
            pltpu.make_async_copy(part, whole.at[pl.ds(at, part.shape[0])], sems.at[i])
        )
        at += part.shape[0]
    for copy in copies:
        copy.start()
    return copies


def list_kernel(slots, owners, pos, own_index, mate_index, lists, counts):
    stride = lists.shape[0] // (SEGMENTS * QUARTERS)
    for place in range(SEGMENTS * QUARTERS):
        counts[place] = 0

    def clear(i, carry):
        lists[i] = 2 * slots
        return carry

    lax.fori_loop(0, lists.shape[0], clear, 0, unroll=16)
    quarter = pos[0]
    for first, index in ((0, own_index), (slots, mate_index)):

        def put(s, carry, first=first, index=index):
            col = index[1, s]
            turn = (col - quarter) & 3
            owner = col >> 2
            late = (owner >= owners // 2).astype(jnp.int32) * (turn == 2).astype(jnp.int32)
            segment = jnp.where(turn == 3, 1, turn + late)
            block = owner + jnp.where(turn == 3, owners, -late * (owners // 2))
            place = segment * QUARTERS + index[0, s]
            n = counts[place]
            lists[place * stride + n] = first + s + (block << 10)
            counts[place] = n + index[2, s]
            return carry

        lax.fori_loop(0, slots, put, 0, unroll=8)
    for place in range(SEGMENTS * QUARTERS):
        lists[place * stride + counts[place]] = 2 * slots


def own_kernel(lists, counts, own_tiles, mate_tiles, x_own, tiles, total, sems):
    copies = collect((own_tiles, mate_tiles), tiles, sems)
    total[...] = jnp.zeros_like(total)
    tiles[tiles.shape[0] - 1] = jnp.zeros(tiles.shape[1:], BF16)
    for copy in copies:
        copy.wait()
    multiply(0, tiles, x_own, lists, counts, total)


def near_kernel(lists, counts, tiles, next_a, next_b, prev_a, prev_b, before, total, blocks, sems):
    copies = collect((next_a, next_b, prev_a, prev_b), blocks, sems)
    del before
    for copy in copies:
        copy.wait()
    multiply(1, tiles, blocks, lists, counts, total)


def far_kernel(lists, counts, tiles, far_a, before, total):
    del before
    multiply(2, tiles, far_a, lists, counts, total)


def last_kernel(lists, counts, tiles, far_b, before, cotangent, out, total, terms, sem):
    load = pltpu.make_async_copy(cotangent, terms, sem)
    load.start()
    total[...] = before[...]
    multiply(3, tiles, far_b, lists, counts, total)
    load.wait()
    members, _, tile = out.shape
    rounded = total[...].astype(BF16).reshape(QUARTERS * tile, tile)
    grad = lax.dot_general(
        rounded, terms[...], (((0,), (0,)), ((), ())), preferred_element_type=F32
    )
    rows = rounded.shape[0] // members
    part = grad.shape[0] // members
    for m in range(members):
        out[m, :rows] = rounded[m * rows : (m + 1) * rows]
        out[m, rows:] = split_wide(grad[m * part : (m + 1) * part]).astype(BF16)


def member_kernel(got, rows_out, out):
    rows = rows_out.shape[0]
    total = jnp.sum(got[...].astype(F32), axis=0).astype(BF16)
    rows_out[...] = total[:rows]
    out[...] = jnp.broadcast_to(total[rows:][None], out.shape)


def grad_kernel(scale, got, rows, out):
    total = jnp.sum(got[...].astype(F32), axis=0) * scale
    packed = jnp.concatenate([rows[...], total.astype(BF16)], axis=0)
    out[...] = jnp.broadcast_to(packed[None], out.shape)


def output_kernel(pos, mine, mate, weight, out_rows, grad_weight, grad_features):
    members, packet, tile = mine.shape
    rows = out_rows.shape[0] // members
    part = grad_weight.shape[0] // members

    def write(forward, backward):
        grad_features[...] = backward[:, :rows].reshape(members * rows, tile)
        words = forward[:, rows:].astype(F32)
        grad_weight[...] = jnp.concatenate(
            [words[:, :part], words[:, part:]], axis=2
        ).reshape(grad_weight.shape)
        aggregated = forward[:, :rows].reshape(members * rows, tile)
        out_rows[...] = jnp.dot(
            aggregated, weight[...], preferred_element_type=F32
        ).astype(BF16)

    pl.when(pos[1] == 0)(lambda: write(mine, mate))
    pl.when(pos[1] == 1)(lambda: write(mate, mine))


def after(value, other):
    return pl.pallas_call(
        lambda *refs: None,
        out_shape=jax.ShapeDtypeStruct(value.shape, value.dtype),
        in_specs=[ANY, ANY],
        out_specs=ANY,
        input_output_aliases={0: 0},
        compiler_params=pltpu.CompilerParams(vmem_limit_bytes=SMALL),
    )(value, other)


def in_hbm(value):
    return pltpu.with_memory_space_constraint(value, pltpu.HBM)


def to_all(value, axis):
    return lax.all_to_all(value, axis, 0, 0, tiled=True)


def local(features, weight, cotangent, adj_values, block_rows, block_cols, block_live):
    owners = lax.axis_size("row")
    quarters = lax.axis_size("x")
    members = lax.axis_size("hi") * quarters
    slots, tile = adj_values.shape[:2]
    width = weight.shape[1]
    nodes = features.shape[0] * owners
    ring = lambda step: [(i, (i + step) % quarters) for i in range(quarters)]
    swap = [(0, 1), (1, 0)]
    rows = features.shape[0] // members
    tail = (weight.shape[0] // members) * (width // tile)
    packet = jax.ShapeDtypeStruct((members, rows + tail, tile), BF16)

    pos = jnp.stack([lax.axis_index("x"), lax.axis_index("core")]).astype(jnp.int32)

    source = kernel_call(
        source_kernel,
        jax.ShapeDtypeStruct((owners, tile, tile), BF16),
        [SMEM, ANY, ANY, ANY],
        scratch=[
            pltpu.VMEM((tile, tile), BF16),
            pltpu.VMEM((tile, width), BF16),
            pltpu.VMEM(weight.shape, BF16),
            pltpu.SemaphoreType.DMA((3,)),
        ],
    )(pos, in_hbm(features), in_hbm(cotangent), in_hbm(weight))
    own_tiles, *index, source = lax.optimization_barrier(
        (adj_values, block_rows, block_cols, block_live, source)
    )
    mate_tiles = lax.ppermute(own_tiles, "core", swap)
    own_index = jnp.stack(index)
    mate_index = lax.ppermute(own_index, "core", swap)
    places = SEGMENTS * QUARTERS
    sums = jax.ShapeDtypeStruct((QUARTERS, tile, tile), F32)
    lists, counts = kernel_call(
        functools.partial(list_kernel, slots, owners),
        (
            jax.ShapeDtypeStruct((places * (2 * slots + GROUP),), jnp.int32),
            jax.ShapeDtypeStruct((places,), jnp.int32),
        ),
        [SMEM, SMEM, SMEM],
        out_specs=(SMEM, SMEM),
    )(pos, own_index, mate_index)
    x_own = after(to_all(source, "row"), counts)

    half = owners // 2
    low, high = x_own[:half], x_own[half:]
    prev_a = lax.ppermute(low, "x", ring(1))
    next_b = lax.ppermute(high, "x", ring(-1))
    prev_b = lax.ppermute(high, "x", ring(1))
    next_a = lax.ppermute(low, "x", ring(-1))
    far_a = lax.ppermute(prev_a, "x", ring(1))
    far_b = lax.ppermute(next_b, "x", ring(-1))
    tiles, total = kernel_call(
        own_kernel,
        (jax.ShapeDtypeStruct((2 * slots + 1, tile, tile), BF16), sums),
        [SMEM, SMEM, ANY, ANY, VMEM],
        scratch=[pltpu.SemaphoreType.DMA((2,))],
    )(lists, counts, in_hbm(adj_values), mate_tiles, x_own)
    total = kernel_call(
        near_kernel,
        sums,
        [SMEM, SMEM] + [VMEM] * 6,
        aliases={7: 0},
        scratch=[
            pltpu.VMEM((2 * owners, tile, tile), BF16),
            pltpu.SemaphoreType.DMA((4,)),
        ],
    )(lists, counts, tiles, next_a, next_b, prev_a, prev_b, total)
    total = kernel_call(far_kernel, sums, [SMEM, SMEM] + [VMEM] * 3, aliases={4: 0})(
        lists, counts, tiles, far_a, total
    )
    partial = kernel_call(
        last_kernel,
        packet,
        [SMEM, SMEM] + [VMEM] * 3 + [ANY],
        scratch=[
            pltpu.VMEM((QUARTERS, tile, tile), F32),
            pltpu.VMEM(cotangent.shape, BF16),
            pltpu.SemaphoreType.DMA,
        ],
    )(lists, counts, tiles, far_b, total, in_hbm(cotangent))

    got = to_all(partial, ("x", "hi"))
    done, terms = kernel_call(
        member_kernel,
        (
            jax.ShapeDtypeStruct((rows, tile), BF16),
            jax.ShapeDtypeStruct((owners, tail, tile), BF16),
        ),
        [VMEM],
    )(got)
    terms = to_all(terms, "row")
    packed = kernel_call(
        functools.partial(grad_kernel, nodes ** (-0.5)), packet, [VMEM, VMEM]
    )(terms, done)
    mine = to_all(packed, ("x", "hi"))
    mate = lax.ppermute(mine, "core", swap)
    return kernel_call(
        output_kernel,
        (
            jax.ShapeDtypeStruct((features.shape[0], width), BF16),
            jax.ShapeDtypeStruct(weight.shape, F32),
            jax.ShapeDtypeStruct(features.shape, BF16),
        ),
        [SMEM, VMEM, VMEM, VMEM],
    )(pos, mine, mate, weight)


def solution(mesh):
    owners, members = mesh.devices.shape
    fine = Mesh(
        mesh.devices.reshape(owners, members // (2 * QUARTERS), QUARTERS, 2),
        ("row", "hi", "x", "core"),
    )
    tiles = ("row", "hi", "x", "core")
    in_specs = (
        P("row", None),
        P(),
        P("row", None),
        P(tiles, None, None),
        P(tiles),
        P(tiles),
        P(tiles),
    )
    out_specs = (P("row", None), P(), P("row", None))
    return jax.shard_map(local, mesh=fine, in_specs=in_specs, out_specs=out_specs, check_vma=False)
```

```python
import functools

import jax
import jax.numpy as jnp
from jax import lax
from jax.experimental import pallas as pl
from jax.experimental.pallas import tpu as pltpu
from jax.sharding import Mesh
from jax.sharding import PartitionSpec as P

BF16 = jnp.bfloat16
F32 = jnp.float32
GROUP = 8
QUARTERS = 4
LIMIT = 12 * 1024 * 1024
SMALL = 1024 * 1024
SEGMENTS = 4
VMEM = pl.BlockSpec(memory_space=pltpu.VMEM)
SMEM = pl.BlockSpec(memory_space=pltpu.SMEM)
ANY = pl.BlockSpec(memory_space=pl.ANY)


def kernel_call(kernel, out_shape, in_specs, out_specs=None, scratch=(), aliases=None):
    if out_specs is None:
        out_specs = jax.tree.map(lambda _: VMEM, out_shape)
    return pl.pallas_call(
        kernel,
        out_shape=out_shape,
        in_specs=in_specs,
        out_specs=out_specs,
        scratch_shapes=scratch,
        input_output_aliases=aliases or {},
        compiler_params=pltpu.CompilerParams(vmem_limit_bytes=LIMIT),
    )


def split_wide(wide):
    half = wide.shape[1] // 2
    return jnp.concatenate([wide[:, :half], wide[:, half:]], axis=0)


def upper_lanes(shape):
    return (lax.broadcasted_iota(jnp.int32, shape, 1) >= shape[1] // 2).astype(jnp.int32)


def two_words(total):
    high = total.astype(BF16)
    low = (total - high.astype(F32)).astype(BF16)
    return jnp.concatenate([high, low], axis=0)


def source_kernel(pos, features, cotangent, weight, out, own_rows, own_terms, factors, sems):
    tile = out.shape[1]
    rows = pl.ds(pl.multiple_of(pos[0] * tile, tile), tile)
    copies = [
        pltpu.make_async_copy(source, target, sems.at[i])
        for i, (source, target) in enumerate(
            (
                (features.at[rows, :], own_rows),
                (cotangent.at[rows, :], own_terms),
                (weight, factors),
            )
        )
    ]
    for copy in copies:
        copy.start()
    for copy in copies:
        copy.wait()
    projected = lax.dot_general(
        own_terms[...], factors[...], (((1,), (1,)), ((), ())), preferred_element_type=F32
    ).astype(BF16)
    kept = jnp.where(
        upper_lanes(out.shape[1:]) == pos[1], own_rows[...].astype(F32), projected.astype(F32)
    ).astype(BF16)
    out[...] = jnp.broadcast_to(kept[None], out.shape)


def multiply(segment, tiles, blocks, lists, counts, total):
    stride = lists.shape[0] // (SEGMENTS * QUARTERS)
    longest = counts[segment * QUARTERS]
    for r in range(1, QUARTERS):
        longest = jnp.maximum(longest, counts[segment * QUARTERS + r])

    def step(g, carry):
        for r in range(QUARTERS):
            at = (segment * QUARTERS + r) * stride + g * GROUP
            words = [lists[at + j] for j in range(GROUP)]
            left = jnp.concatenate([tiles[word & 1023] for word in words], axis=1)
            right = jnp.concatenate([blocks[word >> 10] for word in words], axis=0)
            total[r] += jnp.dot(left, right, preferred_element_type=F32)
        return carry

    lax.fori_loop(0, (longest + (GROUP - 1)) >> 3, step, 0)


def collect(parts, whole, sems):
    copies = []
    at = 0
    for i, part in enumerate(parts):
        copies.append(
            pltpu.make_async_copy(part, whole.at[pl.ds(at, part.shape[0])], sems.at[i])
        )
        at += part.shape[0]
    for copy in copies:
        copy.start()
    return copies


def list_kernel(slots, owners, pos, own_index, mate_index, lists, counts):
    stride = lists.shape[0] // (SEGMENTS * QUARTERS)
    for place in range(SEGMENTS * QUARTERS):
        counts[place] = 0

    def clear(i, carry):
        lists[i] = 2 * slots
        return carry

    lax.fori_loop(0, lists.shape[0], clear, 0, unroll=16)
    quarter = pos[0]
    for first, index in ((0, own_index), (slots, mate_index)):

        def put(s, carry, first=first, index=index):
            col = index[1, s]
            turn = (col - quarter) & 3
            owner = col >> 2
            late = (owner >= owners // 2).astype(jnp.int32) * (turn == 2).astype(jnp.int32)
            segment = jnp.where(turn == 3, 1, turn + late)
            block = owner + jnp.where(turn == 3, owners, -late * (owners // 2))
            place = segment * QUARTERS + index[0, s]
            n = counts[place]
            lists[place * stride + n] = first + s + (block << 10)
            counts[place] = n + index[2, s]
            return carry

        lax.fori_loop(0, slots, put, 0, unroll=8)
    for place in range(SEGMENTS * QUARTERS):
        lists[place * stride + counts[place]] = 2 * slots


def own_kernel(lists, counts, own_tiles, mate_tiles, x_own, tiles, total, sems):
    copies = collect((own_tiles, mate_tiles), tiles, sems)
    total[...] = jnp.zeros_like(total)
    tiles[tiles.shape[0] - 1] = jnp.zeros(tiles.shape[1:], BF16)
    for copy in copies:
        copy.wait()
    multiply(0, tiles, x_own, lists, counts, total)


def near_kernel(lists, counts, tiles, next_a, next_b, prev_a, prev_b, before, total, blocks, sems):
    copies = collect((next_a, next_b, prev_a, prev_b), blocks, sems)
    del before
    for copy in copies:
        copy.wait()
    multiply(1, tiles, blocks, lists, counts, total)


def far_kernel(lists, counts, tiles, far_a, before, total):
    del before
    multiply(2, tiles, far_a, lists, counts, total)


def last_kernel(pos, lists, counts, tiles, far_b, before, cotangent, out, total, terms, sem):
    load = pltpu.make_async_copy(cotangent, terms, sem)
    load.start()
    total[...] = before[...]
    multiply(3, tiles, far_b, lists, counts, total)
    load.wait()
    members, _, tile = out.shape
    rounded = total[...].astype(BF16).reshape(QUARTERS * tile, tile)
    grad = lax.dot_general(
        rounded, terms[...], (((0,), (0,)), ((), ())), preferred_element_type=F32
    )
    half = grad.shape[0] // 2
    grad = split_wide(jnp.where(pos[1] == 0, grad[:half], grad[half:]))
    rows = rounded.shape[0] // members
    part = grad.shape[0] // members
    for m in range(members):
        out[m, :rows] = rounded[m * rows : (m + 1) * rows]
        out[m, rows:] = grad[m * part : (m + 1) * part].astype(BF16)


def member_kernel(got, rows_out, out):
    rows = rows_out.shape[0]
    total = jnp.sum(got[...].astype(F32), axis=0)
    rows_out[...] = total[:rows].astype(BF16)
    out[...] = jnp.broadcast_to(two_words(total[rows:])[None], out.shape)


def grad_kernel(scale, got, rows, out):
    total = jnp.sum(got[...].astype(F32), axis=0)
    half = total.shape[0] // 2
    total = (total[:half] + total[half:]) * scale
    packed = jnp.concatenate([rows[...].astype(F32), total], axis=0).astype(BF16)
    out[...] = jnp.broadcast_to(packed[None], out.shape)


def output_kernel(pos, mine, mate, weight, out_rows, grad_weight, grad_features):
    members, packet, tile = mine.shape
    rows = out_rows.shape[0] // members
    half = grad_weight.shape[0] // 2

    def write(lower, upper):
        first = lower[:, :rows].reshape(members * rows, tile).astype(F32)
        second = upper[:, :rows].reshape(members * rows, tile).astype(F32)
        is_upper = upper_lanes(first.shape) == 1
        grad_features[...] = jnp.where(is_upper, first, second).astype(BF16)
        aggregated = jnp.where(is_upper, second, first).astype(BF16)
        out_rows[...] = jnp.dot(
            aggregated, weight[...], preferred_element_type=F32
        ).astype(BF16)
        for i, packets in enumerate((lower, upper)):
            words = packets[:, rows:].astype(F32).reshape(2 * half, tile)
            grad_weight[i * half : (i + 1) * half] = jnp.concatenate(
                [words[:half], words[half:]], axis=1
            )

    pl.when(pos[1] == 0)(lambda: write(mine, mate))
    pl.when(pos[1] == 1)(lambda: write(mate, mine))


def after(value, other):
    return pl.pallas_call(
        lambda *refs: None,
        out_shape=jax.ShapeDtypeStruct(value.shape, value.dtype),
        in_specs=[ANY, ANY],
        out_specs=ANY,
        input_output_aliases={0: 0},
        compiler_params=pltpu.CompilerParams(vmem_limit_bytes=SMALL),
    )(value, other)


def in_hbm(value):
    return pltpu.with_memory_space_constraint(value, pltpu.HBM)


def to_all(value, axis):
    return lax.all_to_all(value, axis, 0, 0, tiled=True)


def local(features, weight, cotangent, adj_values, block_rows, block_cols, block_live):
    owners = lax.axis_size("row")
    quarters = lax.axis_size("x")
    members = lax.axis_size("hi") * quarters
    slots, tile = adj_values.shape[:2]
    width = weight.shape[1]
    nodes = features.shape[0] * owners
    ring = lambda step: [(i, (i + step) % quarters) for i in range(quarters)]
    swap = [(0, 1), (1, 0)]
    rows = features.shape[0] // members
    tail = (weight.shape[0] // 2) * (width // tile) // members
    packet = jax.ShapeDtypeStruct((members, rows + tail, tile), BF16)

    pos = jnp.stack([lax.axis_index("x"), lax.axis_index("core")]).astype(jnp.int32)

    source = kernel_call(
        source_kernel,
        jax.ShapeDtypeStruct((owners, tile, tile), BF16),
        [SMEM, ANY, ANY, ANY],
        scratch=[
            pltpu.VMEM((tile, tile), BF16),
            pltpu.VMEM((tile, width), BF16),
            pltpu.VMEM(weight.shape, BF16),
            pltpu.SemaphoreType.DMA((3,)),
        ],
    )(pos, in_hbm(features), in_hbm(cotangent), in_hbm(weight))
    own_tiles, *index, source = lax.optimization_barrier(
        (adj_values, block_rows, block_cols, block_live, source)
    )
    mate_tiles = lax.ppermute(own_tiles, "core", swap)
    own_index = jnp.stack(index)
    mate_index = lax.ppermute(own_index, "core", swap)
    places = SEGMENTS * QUARTERS
    sums = jax.ShapeDtypeStruct((QUARTERS, tile, tile), F32)
    lists, counts = kernel_call(
        functools.partial(list_kernel, slots, owners),
        (
            jax.ShapeDtypeStruct((places * (2 * slots + GROUP),), jnp.int32),
            jax.ShapeDtypeStruct((places,), jnp.int32),
        ),
        [SMEM, SMEM, SMEM],
        out_specs=(SMEM, SMEM),
    )(pos, own_index, mate_index)
    x_own = after(to_all(source, "row"), counts)

    half = owners // 2
    low, high = x_own[:half], x_own[half:]
    prev_a = lax.ppermute(low, "x", ring(1))
    next_b = lax.ppermute(high, "x", ring(-1))
    prev_b = lax.ppermute(high, "x", ring(1))
    next_a = lax.ppermute(low, "x", ring(-1))
    far_a = lax.ppermute(prev_a, "x", ring(1))
    far_b = lax.ppermute(next_b, "x", ring(-1))
    tiles, total = kernel_call(
        own_kernel,
        (jax.ShapeDtypeStruct((2 * slots + 1, tile, tile), BF16), sums),
        [SMEM, SMEM, ANY, ANY, VMEM],
        scratch=[pltpu.SemaphoreType.DMA((2,))],
    )(lists, counts, in_hbm(adj_values), mate_tiles, x_own)
    total = kernel_call(
        near_kernel,
        sums,
        [SMEM, SMEM] + [VMEM] * 6,
        aliases={7: 0},
        scratch=[
            pltpu.VMEM((2 * owners, tile, tile), BF16),
            pltpu.SemaphoreType.DMA((4,)),
        ],
    )(lists, counts, tiles, next_a, next_b, prev_a, prev_b, total)
    total = kernel_call(far_kernel, sums, [SMEM, SMEM] + [VMEM] * 3, aliases={4: 0})(
        lists, counts, tiles, far_a, total
    )
    partial = kernel_call(
        last_kernel,
        packet,
        [SMEM] * 3 + [VMEM] * 3 + [ANY],
        scratch=[
            pltpu.VMEM((QUARTERS, tile, tile), F32),
            pltpu.VMEM(cotangent.shape, BF16),
            pltpu.SemaphoreType.DMA,
        ],
    )(pos, lists, counts, tiles, far_b, total, in_hbm(cotangent))

    got = to_all(partial, ("x", "hi"))
    done, terms = kernel_call(
        member_kernel,
        (
            jax.ShapeDtypeStruct((rows, tile), BF16),
            jax.ShapeDtypeStruct((owners, 2 * tail, tile), BF16),
        ),
        [VMEM],
    )(got)
    terms = to_all(terms, "row")
    packed = kernel_call(
        functools.partial(grad_kernel, nodes ** (-0.5)), packet, [VMEM, VMEM]
    )(terms, done)
    mine = to_all(packed, ("x", "hi"))
    mate = lax.ppermute(mine, "core", swap)
    return kernel_call(
        output_kernel,
        (
            jax.ShapeDtypeStruct((features.shape[0], width), BF16),
            jax.ShapeDtypeStruct(weight.shape, F32),
            jax.ShapeDtypeStruct(features.shape, BF16),
        ),
        [SMEM, VMEM, VMEM, VMEM],
    )(pos, mine, mate, weight)


def solution(mesh):
    owners, members = mesh.devices.shape
    fine = Mesh(
        mesh.devices.reshape(owners, members // (2 * QUARTERS), QUARTERS, 2),
        ("row", "hi", "x", "core"),
    )
    tiles = ("row", "hi", "x", "core")
    in_specs = (
        P("row", None),
        P(),
        P("row", None),
        P(tiles, None, None),
        P(tiles),
        P(tiles),
        P(tiles),
    )
    out_specs = (P("row", None), P(), P("row", None))
    return jax.shard_map(local, mesh=fine, in_specs=in_specs, out_specs=out_specs, check_vma=False)
```

```python
import functools

import jax
import jax.numpy as jnp
from jax import lax
from jax.experimental import pallas as pl
from jax.experimental.pallas import tpu as pltpu
from jax.sharding import Mesh
from jax.sharding import PartitionSpec as P

BF16 = jnp.bfloat16
F32 = jnp.float32
GROUP = 8
QUARTERS = 4
LIMIT = 12 * 1024 * 1024
SMALL = 1024 * 1024
SEGMENTS = 4
VMEM = pl.BlockSpec(memory_space=pltpu.VMEM)
SMEM = pl.BlockSpec(memory_space=pltpu.SMEM)
ANY = pl.BlockSpec(memory_space=pl.ANY)


def kernel_call(kernel, out_shape, in_specs, out_specs=None, scratch=(), aliases=None):
    if out_specs is None:
        out_specs = jax.tree.map(lambda _: VMEM, out_shape)
    return pl.pallas_call(
        kernel,
        out_shape=out_shape,
        in_specs=in_specs,
        out_specs=out_specs,
        scratch_shapes=scratch,
        input_output_aliases=aliases or {},
        compiler_params=pltpu.CompilerParams(vmem_limit_bytes=LIMIT),
    )


def split_wide(wide):
    half = wide.shape[1] // 2
    return jnp.concatenate([wide[:, :half], wide[:, half:]], axis=0)


def upper_lanes(shape):
    return (lax.broadcasted_iota(jnp.int32, shape, 1) >= shape[1] // 2).astype(jnp.int32)


def source_kernel(pos, features, cotangent, weight, out, own_rows, own_terms, factors, sems):
    tile = out.shape[1]
    rows = pl.ds(pl.multiple_of(pos[0] * tile, tile), tile)
    copies = [
        pltpu.make_async_copy(source, target, sems.at[i])
        for i, (source, target) in enumerate(
            (
                (features.at[rows, :], own_rows),
                (cotangent.at[rows, :], own_terms),
                (weight, factors),
            )
        )
    ]
    for copy in copies:
        copy.start()
    for copy in copies:
        copy.wait()
    projected = lax.dot_general(
        own_terms[...], factors[...], (((1,), (1,)), ((), ())), preferred_element_type=F32
    ).astype(BF16)
    kept = jnp.where(
        upper_lanes(out.shape[1:]) == pos[1], own_rows[...].astype(F32), projected.astype(F32)
    ).astype(BF16)
    out[...] = jnp.broadcast_to(kept[None], out.shape)


def multiply(segment, tiles, blocks, lists, counts, total):
    stride = lists.shape[0] // (SEGMENTS * QUARTERS)
    longest = counts[segment * QUARTERS]
    for r in range(1, QUARTERS):
        longest = jnp.maximum(longest, counts[segment * QUARTERS + r])

    def step(g, carry):
        for r in range(QUARTERS):
            at = (segment * QUARTERS + r) * stride + g * GROUP
            words = [lists[at + j] for j in range(GROUP)]
            left = jnp.concatenate([tiles[word & 1023] for word in words], axis=1)
            right = jnp.concatenate([blocks[word >> 10] for word in words], axis=0)
            total[r] += jnp.dot(left, right, preferred_element_type=F32)
        return carry

    lax.fori_loop(0, (longest + (GROUP - 1)) >> 3, step, 0)


def collect(parts, whole, sems):
    copies = []
    at = 0
    for i, part in enumerate(parts):
        copies.append(
            pltpu.make_async_copy(part, whole.at[pl.ds(at, part.shape[0])], sems.at[i])
        )
        at += part.shape[0]
    for copy in copies:
        copy.start()
    return copies


def list_kernel(slots, owners, pos, own_index, mate_index, lists, counts):
    stride = lists.shape[0] // (SEGMENTS * QUARTERS)
    for place in range(SEGMENTS * QUARTERS):
        counts[place] = 0

    def clear(i, carry):
        lists[i] = 2 * slots
        return carry

    lax.fori_loop(0, lists.shape[0], clear, 0, unroll=16)
    quarter = pos[0]
    for first, index in ((0, own_index), (slots, mate_index)):

        def put(s, carry, first=first, index=index):
            col = index[1, s]
            turn = (col - quarter) & 3
            owner = col >> 2
            late = (owner >= owners // 2).astype(jnp.int32) * (turn == 2).astype(jnp.int32)
            segment = jnp.where(turn == 3, 1, turn + late)
            block = owner + jnp.where(turn == 3, owners, -late * (owners // 2))
            place = segment * QUARTERS + index[0, s]
            n = counts[place]
            lists[place * stride + n] = first + s + (block << 10)
            counts[place] = n + index[2, s]
            return carry

        lax.fori_loop(0, slots, put, 0, unroll=8)
    for place in range(SEGMENTS * QUARTERS):
        lists[place * stride + counts[place]] = 2 * slots


def own_kernel(lists, counts, own_tiles, mate_tiles, x_own, tiles, total, sems):
    copies = collect((own_tiles, mate_tiles), tiles, sems)
    total[...] = jnp.zeros_like(total)
    tiles[tiles.shape[0] - 1] = jnp.zeros(tiles.shape[1:], BF16)
    for copy in copies:
        copy.wait()
    multiply(0, tiles, x_own, lists, counts, total)


def near_kernel(lists, counts, tiles, next_a, next_b, prev_a, prev_b, before, total, blocks, sems):
    copies = collect((next_a, next_b, prev_a, prev_b), blocks, sems)
    del before
    for copy in copies:
        copy.wait()
    multiply(1, tiles, blocks, lists, counts, total)


def far_kernel(lists, counts, tiles, far_a, before, total):
    del before
    multiply(2, tiles, far_a, lists, counts, total)


def last_kernel(pos, lists, counts, tiles, far_b, before, cotangent, out, total, terms, sem):
    load = pltpu.make_async_copy(cotangent, terms, sem)
    load.start()
    total[...] = before[...]
    multiply(3, tiles, far_b, lists, counts, total)
    load.wait()
    members, _, tile = out.shape
    rounded = total[...].astype(BF16).reshape(QUARTERS * tile, tile)
    grad = lax.dot_general(
        rounded, terms[...], (((0,), (0,)), ((), ())), preferred_element_type=F32
    )
    half = grad.shape[0] // 2
    grad = split_wide(jnp.where(pos[1] == 0, grad[:half], grad[half:]))
    rows = rounded.shape[0] // members
    part = grad.shape[0] // members
    for m in range(members):
        out[m, :rows] = rounded[m * rows : (m + 1) * rows]
        out[m, rows:] = grad[m * part : (m + 1) * part].astype(BF16)


def member_kernel(got, rows_out, out):
    rows = rows_out.shape[0]
    total = jnp.sum(got[...].astype(F32), axis=0)
    rows_out[...] = total[:rows].astype(BF16)
    out[...] = jnp.broadcast_to(total[rows:].astype(BF16)[None], out.shape)


def grad_kernel(scale, got, rows, out):
    total = jnp.sum(got[...].astype(F32), axis=0) * scale
    packed = jnp.concatenate([rows[...].astype(F32), total], axis=0).astype(BF16)
    out[...] = jnp.broadcast_to(packed[None], out.shape)


def output_kernel(pos, mine, mate, weight, out_rows, grad_weight, grad_features):
    members, packet, tile = mine.shape
    rows = out_rows.shape[0] // members
    half = grad_weight.shape[0] // 2

    def write(lower, upper):
        first = lower[:, :rows].reshape(members * rows, tile).astype(F32)
        second = upper[:, :rows].reshape(members * rows, tile).astype(F32)
        is_upper = upper_lanes(first.shape) == 1
        grad_features[...] = jnp.where(is_upper, first, second).astype(BF16)
        aggregated = jnp.where(is_upper, second, first).astype(BF16)
        out_rows[...] = jnp.dot(
            aggregated, weight[...], preferred_element_type=F32
        ).astype(BF16)
        for i, packets in enumerate((lower, upper)):
            words = packets[:, rows:].astype(F32).reshape(2 * half, tile)
            grad_weight[i * half : (i + 1) * half] = jnp.concatenate(
                [words[:half], words[half:]], axis=1
            )

    pl.when(pos[1] == 0)(lambda: write(mine, mate))
    pl.when(pos[1] == 1)(lambda: write(mate, mine))


def after(value, other):
    return pl.pallas_call(
        lambda *refs: None,
        out_shape=jax.ShapeDtypeStruct(value.shape, value.dtype),
        in_specs=[ANY, ANY],
        out_specs=ANY,
        input_output_aliases={0: 0},
        compiler_params=pltpu.CompilerParams(vmem_limit_bytes=SMALL),
    )(value, other)


def in_hbm(value):
    return pltpu.with_memory_space_constraint(value, pltpu.HBM)


def to_all(value, axis):
    return lax.all_to_all(value, axis, 0, 0, tiled=True)


def local(features, weight, cotangent, adj_values, block_rows, block_cols, block_live):
    owners = lax.axis_size("row")
    quarters = lax.axis_size("x")
    members = lax.axis_size("hi") * quarters
    slots, tile = adj_values.shape[:2]
    width = weight.shape[1]
    nodes = features.shape[0] * owners
    ring = lambda step: [(i, (i + step) % quarters) for i in range(quarters)]
    swap = [(0, 1), (1, 0)]
    rows = features.shape[0] // members
    tail = (weight.shape[0] // 2) * (width // tile) // members
    packet = jax.ShapeDtypeStruct((members, rows + tail, tile), BF16)

    pos = jnp.stack([lax.axis_index("x"), lax.axis_index("core")]).astype(jnp.int32)

    source = kernel_call(
        source_kernel,
        jax.ShapeDtypeStruct((owners, tile, tile), BF16),
        [SMEM, ANY, ANY, ANY],
        scratch=[
            pltpu.VMEM((tile, tile), BF16),
            pltpu.VMEM((tile, width), BF16),
            pltpu.VMEM(weight.shape, BF16),
            pltpu.SemaphoreType.DMA((3,)),
        ],
    )(pos, in_hbm(features), in_hbm(cotangent), in_hbm(weight))
    own_tiles, *index, source = lax.optimization_barrier(
        (adj_values, block_rows, block_cols, block_live, source)
    )
    mate_tiles = lax.ppermute(own_tiles, "core", swap)
    own_index = jnp.stack(index)
    mate_index = lax.ppermute(own_index, "core", swap)
    places = SEGMENTS * QUARTERS
    sums = jax.ShapeDtypeStruct((QUARTERS, tile, tile), F32)
    lists, counts = kernel_call(
        functools.partial(list_kernel, slots, owners),
        (
            jax.ShapeDtypeStruct((places * (2 * slots + GROUP),), jnp.int32),
            jax.ShapeDtypeStruct((places,), jnp.int32),
        ),
        [SMEM, SMEM, SMEM],
        out_specs=(SMEM, SMEM),
    )(pos, own_index, mate_index)
    x_own = after(to_all(source, "row"), counts)

    half = owners // 2
    low, high = x_own[:half], x_own[half:]
    prev_a = lax.ppermute(low, "x", ring(1))
    next_b = lax.ppermute(high, "x", ring(-1))
    prev_b = lax.ppermute(high, "x", ring(1))
    next_a = lax.ppermute(low, "x", ring(-1))
    far_a = lax.ppermute(prev_a, "x", ring(1))
    far_b = lax.ppermute(next_b, "x", ring(-1))
    tiles, total = kernel_call(
        own_kernel,
        (jax.ShapeDtypeStruct((2 * slots + 1, tile, tile), BF16), sums),
        [SMEM, SMEM, ANY, ANY, VMEM],
        scratch=[pltpu.SemaphoreType.DMA((2,))],
    )(lists, counts, in_hbm(adj_values), mate_tiles, x_own)
    total = kernel_call(
        near_kernel,
        sums,
        [SMEM, SMEM] + [VMEM] * 6,
        aliases={7: 0},
        scratch=[
            pltpu.VMEM((2 * owners, tile, tile), BF16),
            pltpu.SemaphoreType.DMA((4,)),
        ],
    )(lists, counts, tiles, next_a, next_b, prev_a, prev_b, total)
    total = kernel_call(far_kernel, sums, [SMEM, SMEM] + [VMEM] * 3, aliases={4: 0})(
        lists, counts, tiles, far_a, total
    )
    partial = kernel_call(
        last_kernel,
        packet,
        [SMEM] * 3 + [VMEM] * 3 + [ANY],
        scratch=[
            pltpu.VMEM((QUARTERS, tile, tile), F32),
            pltpu.VMEM(cotangent.shape, BF16),
            pltpu.SemaphoreType.DMA,
        ],
    )(pos, lists, counts, tiles, far_b, total, in_hbm(cotangent))

    got = to_all(partial, ("x", "hi"))
    done, terms = kernel_call(
        member_kernel,
        (
            jax.ShapeDtypeStruct((rows, tile), BF16),
            jax.ShapeDtypeStruct((owners, tail, tile), BF16),
        ),
        [VMEM],
    )(got)
    terms = to_all(terms, "row")
    packed = kernel_call(
        functools.partial(grad_kernel, nodes ** (-0.5)), packet, [VMEM, VMEM]
    )(terms, done)
    mine = to_all(packed, ("x", "hi"))
    mate = lax.ppermute(mine, "core", swap)
    return kernel_call(
        output_kernel,
        (
            jax.ShapeDtypeStruct((features.shape[0], width), BF16),
            jax.ShapeDtypeStruct(weight.shape, F32),
            jax.ShapeDtypeStruct(features.shape, BF16),
        ),
        [SMEM, VMEM, VMEM, VMEM],
    )(pos, mine, mate, weight)


def solution(mesh):
    owners, members = mesh.devices.shape
    fine = Mesh(
        mesh.devices.reshape(owners, members // (2 * QUARTERS), QUARTERS, 2),
        ("row", "hi", "x", "core"),
    )
    tiles = ("row", "hi", "x", "core")
    in_specs = (
        P("row", None),
        P(),
        P("row", None),
        P(tiles, None, None),
        P(tiles),
        P(tiles),
        P(tiles),
    )
    out_specs = (P("row", None), P(), P("row", None))
    return jax.shard_map(local, mesh=fine, in_specs=in_specs, out_specs=out_specs, check_vma=False)
```
